32 devices in a mesh: patch: 2 (over core), lat: 2 (over y), lon: 8 (over z, x).
Axes of the slice: x: 2, y: 2, z: 4, core: 2. Of those that a mesh axis runs over, the one named last changes fastest.
Arguments:
- velocity: float32 [2, 3, 32, 64, 128], P('patch', None, 'lat', 'lon'), may hold values from -6 to 6
- forcing: float32 [2, 3, 32, 64, 128], P('patch', None, 'lat', 'lon'), may hold values from -3 to 3
- viscosity: float32 [2, 32, 64, 128], P('patch', 'lat', 'lon'), may hold values from 1 to 10
- ghost_slots: int32 [2, 192], P('patch'), may hold values from 0 to 191, each once within a row
- corner_rows: int32 [2, 2, 96], P('patch', 'lat', 'lon'), may hold values from 0 to 15
- corner_cols: int32 [2, 2, 96], P('patch', 'lat', 'lon'), may hold values from 0 to 7
- corner_weights: float32 [2, 2, 4, 96], P('patch', 'lat', None, 'lon'), may hold values from 0 to 1, as said below
Outputs:
- new_velocity: float32 [2, 3, 32, 64, 128], P('patch', None, 'lat', 'lon')
- residual: float32 [2, 3, 32, 64, 128], P('patch', None, 'lat', 'lon')
The draws below stay inside these ranges and needn't reach their ends.
Inputs may be any that keep to these rules, and one draw needn't show every extreme that they name: `ghost_slots`: each row names every slot of the other patch exactly once. `corner_rows`: the row below the corner is read too, from the next device or as zero beyond the patch. `corner_cols`: the column after the corner is read too, from the next device or as zero beyond the patch. `corner_weights`: the four weights of a slot are (1 - s)(1 - t), s(1 - t), (1 - s)t and st for some s and t in [0, 1).
All inputs are finite; a program needn't handle non-finite values.
Results may differ from the reference program's by a relative error of at most 0.0001.
Values sent between devices are 32-bit elements; how exact they have to be, the bound alone decides.
A program may use at most 64 MiB of HBM per device.

```python
import math
import jax
import jax.numpy as jnp

CLAT = 16
CLON = 8
R = 128
SWEEPS = 2
COARSE = 8
NLAT = 32
NLON = 64
G = 192
Q = 12
N_PATCH = 2
N_LAT = 2
N_LON = 8


def draw_forcing(key, part):
    array_shape = (N_PATCH, 3, NLAT, NLON, R)
    return jax.random.uniform(key, array_shape, jnp.float32, -3.0, 3.0)


def draw_corner_weights(key, part):
    array_shape = (N_PATCH, N_LAT, 1, N_LON * Q)
    along_lat = jax.random.uniform(jax.random.fold_in(key, 11), array_shape, jnp.float32)
    along_lon = jax.random.uniform(jax.random.fold_in(key, 12), array_shape, jnp.float32)
    return jnp.concatenate([(1.0 - along_lat) * (1.0 - along_lon), along_lat * (1.0 - along_lon), (1.0 - along_lat) * along_lon, along_lat * along_lon], axis=2)


def with_ends(result, rng, low, largest):
    index_at = [jax.random.randint(jax.random.fold_in(rng, axis), (), 0, length) for axis, length in enumerate(result.shape)]
    main_axis = result.shape.index(max(result.shape))
    next_to = index_at[:main_axis] + [(index_at[main_axis] + 1) % result.shape[main_axis]] + index_at[main_axis + 1:]
    return result.at[tuple(index_at)].set(low).at[tuple(next_to)].set(largest)


def block_levels(own_key, shape, split, smallest, top_value):
    gain = 1.0
    for position, parts in split:
        heights = jax.random.uniform(jax.random.fold_in(jax.random.fold_in(own_key, 6), position), (parts,), jnp.float32, smallest / len(split), top_value / len(split))
        gain = gain * jnp.repeat(jnp.exp(heights), shape[position] // parts).reshape((-1,) + (1,) * (len(shape) - 1 - position))
    return gain


def gaussian(own_key, dims, deviation, most, cuts=(), kind=jnp.bfloat16):
    array = deviation * jax.random.normal(own_key, dims, jnp.float32)
    if cuts:
        array = array * block_levels(own_key, dims, cuts, -0.22, 0.18)
    return jnp.clip(array, -most, most).astype(kind)


def setup_inputs(seed: int = 0) -> dict:
    key_list = jax.random.split(jax.random.key(seed), 8)
    velocity = gaussian(key_list[0], (N_PATCH, 3, NLAT, NLON, R), 1.0, 6.0, ((0, 2), (2, 2), (3, 8)), jnp.float32)
    forcing = draw_forcing(jax.random.fold_in(key_list[7], 71), 0)
    viscosity = jnp.clip(jnp.exp(math.log(10.0) - 2.3025851 * jax.random.uniform(key_list[2], (N_PATCH, NLAT, NLON, R), jnp.float32) ** block_levels(key_list[2], (N_PATCH, NLAT, NLON, R), ((0, 2), (1, 2), (2, 8)), -0.2, 0.2)), 1.0, 10.0)
    ghost_slots = jax.vmap(lambda own: jax.random.permutation(own, G))(jax.random.split(key_list[3], N_PATCH)).reshape((N_PATCH, G)).astype(jnp.int32)
    corner_rows = with_ends(jax.random.randint(key_list[4], (N_PATCH, N_LAT, N_LON * Q), 0, CLAT), jax.random.fold_in(key_list[4], 1), 0, CLAT - 1).astype(jnp.int32)
    corner_cols = with_ends(jax.random.randint(key_list[5], (N_PATCH, N_LAT, N_LON * Q), 0, CLON), jax.random.fold_in(key_list[5], 1), 0, CLON - 1).astype(jnp.int32)
    corner_weights = draw_corner_weights(jax.random.fold_in(key_list[7], 71), 0)
    return {"velocity": velocity, "forcing": forcing, "viscosity": viscosity, "ghost_slots": ghost_slots, "corner_rows": corner_rows, "corner_cols": corner_cols, "corner_weights": corner_weights}


RELAX = 0.8


def face_terms(padded_visc, weight_scale):
    centre = padded_visc[1:-1, 1:-1, 1:-1]
    return (weight_scale * (centre + padded_visc[:-2, 1:-1, 1:-1]),
            weight_scale * (centre + padded_visc[2:, 1:-1, 1:-1]),
            weight_scale * (centre + padded_visc[1:-1, :-2, 1:-1]),
            weight_scale * (centre + padded_visc[1:-1, 2:, 1:-1]),
            weight_scale * (centre + padded_visc[1:-1, 1:-1, :-2]),
            weight_scale * (centre + padded_visc[1:-1, 1:-1, 2:]))


def diagonal_of(face_coefs):
    return face_coefs[0] + face_coefs[1] + face_coefs[2] + face_coefs[3] + face_coefs[4] + face_coefs[5]


def neighbour_sum(padded, face_coefs):
    summed = face_coefs[0] * padded[:, :-2, 1:-1, 1:-1]
    summed = summed + face_coefs[1] * padded[:, 2:, 1:-1, 1:-1]
    summed = summed + face_coefs[2] * padded[:, 1:-1, :-2, 1:-1]
    summed = summed + face_coefs[3] * padded[:, 1:-1, 2:, 1:-1]
    summed = summed + face_coefs[4] * padded[:, 1:-1, 1:-1, :-2]
    summed = summed + face_coefs[5] * padded[:, 1:-1, 1:-1, 2:]
    return summed


def bilinear(weight_rows, corner_list):
    summed = weight_rows[0][None, :, None] * corner_list[0]
    summed = summed + weight_rows[1][None, :, None] * corner_list[1]
    summed = summed + weight_rows[2][None, :, None] * corner_list[2]
    summed = summed + weight_rows[3][None, :, None] * corner_list[3]
    return summed


def interpolants(velocity_patch, rows_given, cols_given, weights_given):
    padded = jnp.pad(velocity_patch, ((0, 0), (0, 1), (0, 1), (0, 0)))
    slot_count = N_LAT * N_LON * Q
    slot_ids = jnp.arange(slot_count, dtype=jnp.int32)
    lat_block = slot_ids // (N_LON * Q)
    lon_block = (slot_ids // Q) % N_LON
    row_index = lat_block * CLAT + rows_given.reshape(-1).astype(jnp.int32)
    col_index = lon_block * CLON + cols_given.reshape(-1).astype(jnp.int32)
    weight_rows = jnp.transpose(weights_given, (1, 0, 2)).reshape(4, slot_count)
    corner_list = (padded[:, row_index, col_index], padded[:, row_index + 1, col_index],
                   padded[:, row_index, col_index + 1], padded[:, row_index + 1, col_index + 1])
    return bilinear(weight_rows, corner_list)


def with_loop(velocity_patch, ghost_loop):
    lat_cells = velocity_patch.shape[1]
    lon_cells = velocity_patch.shape[2]
    padded = jnp.pad(velocity_patch, ((0, 0), (1, 1), (1, 1), (1, 1)))
    padded = padded.at[:, 0, 1:-1, 1:-1].set(ghost_loop[:, :lon_cells])
    padded = padded.at[:, -1, 1:-1, 1:-1].set(ghost_loop[:, lon_cells:2 * lon_cells])
    padded = padded.at[:, 1:-1, 0, 1:-1].set(ghost_loop[:, 2 * lon_cells:2 * lon_cells + lat_cells])
    padded = padded.at[:, 1:-1, -1, 1:-1].set(ghost_loop[:, 2 * lon_cells + lat_cells:])
    return padded


def reference(velocity, forcing, viscosity, ghost_slots, corner_rows, corner_cols, corner_weights):
    lat_cells = CLAT * N_LAT
    lon_cells = CLON * N_LON
    slot_values = [interpolants(velocity[patch_index], corner_rows[patch_index], corner_cols[patch_index],
                                corner_weights[patch_index]) for patch_index in range(N_PATCH)]
    parity = (jnp.arange(lat_cells)[:, None, None] + jnp.arange(lon_cells)[None, :, None]
              + jnp.arange(R)[None, None, :]) % 2
    new_fields = []
    residuals = []
    for patch_index in range(N_PATCH):
        ghost_loop = slot_values[N_PATCH - 1 - patch_index][:, ghost_slots[patch_index], :]
        force_patch = forcing[patch_index]
        viscous_patch = viscosity[patch_index]
        face_coefs = face_terms(jnp.pad(viscous_patch, 1, mode="edge"), 0.5)
        diagonal = diagonal_of(face_coefs)
        current = velocity[patch_index]
        for sweep_index in range(SWEEPS):
            for colour in range(2):
                relaxed = (force_patch + neighbour_sum(with_loop(current, ghost_loop), face_coefs)) / diagonal
                current = jnp.where((parity == colour)[None], relaxed, current)
        residual_field = force_patch - (diagonal * current - neighbour_sum(with_loop(current, ghost_loop), face_coefs))
        coarse_rhs = residual_field.reshape(3, lat_cells // 2, 2, lon_cells // 2, 2, R // 2, 2).mean(axis=(2, 4, 6))
        coarse_visc = jnp.pad(viscous_patch, 2, mode="edge").reshape(
            lat_cells // 2 + 2, 2, lon_cells // 2 + 2, 2, R // 2 + 2, 2).mean(axis=(1, 3, 5))
        coarse_coefs = face_terms(coarse_visc, 0.125)
        coarse_diag = diagonal_of(coarse_coefs)
        coarse_error = RELAX * coarse_rhs / coarse_diag
        for turn_index in range(COARSE - 1):
            padded = jnp.pad(coarse_error, ((0, 0), (1, 1), (1, 1), (1, 1)))
            coarse_error = coarse_error + RELAX * (coarse_rhs - (coarse_diag * coarse_error
                                                                - neighbour_sum(padded, coarse_coefs))) / coarse_diag
        correction = jnp.repeat(jnp.repeat(jnp.repeat(coarse_error, 2, axis=1), 2, axis=2), 2, axis=3)
        new_fields.append(current + correction)
        residuals.append(residual_field)
    return jnp.stack(new_fields), jnp.stack(residuals)
```

```python
import functools
import jax
import jax.numpy as jnp
from jax import lax
from jax.experimental import pallas as pl
from jax.experimental.pallas import tpu as pltpu
from jax.sharding import PartitionSpec as P

SWEEPS = 2
COARSE = 8
RELAX = 0.8
MESH = pl.DeviceIdType.MESH


def remote(src, dst, send_sem, recv_sem, device):
    return pltpu.make_async_remote_copy(
        src_ref=src, dst_ref=dst, send_sem=send_sem, recv_sem=recv_sem,
        device_id=device, device_id_type=MESH)


def kernel(sizes, vel, force, visc, slots, rows_in, cols_in, weights, new_out, res_out,
           v, ff, cf, halo, halo_v, srow, rrow, scol, rcol, ssem, rsem,
           sdiag, rdiag, dsem, view, mixed, gathered, gsend, grecv, grow, gcol,
           cvs_row, cvr_row, cvs_col, cvr_col, cvssem, cvrsem,
           ce, cb, cc, chalo, chalo_v, csrow, crrow, cscol, crcol, cssem, crsem):
    rb, cbk, lev, nlat, nlon, q, qrows = sizes
    hr = rb // 2
    n = nlat * nlon
    lat = lax.axis_index("lat")
    lon = lax.axis_index("lon")
    patch = lax.axis_index("patch")
    other = 1 - patch
    me = lat * nlon + lon
    has = (lat > 0, lat < nlat - 1, lon > 0, lon < nlon - 1)
    dev = ({"lat": lat - 1}, {"lat": lat + 1}, {"lon": lon - 1}, {"lon": lon + 1})
    dev_ul = {"lat": lat - 1, "lon": lon - 1}
    dev_dr = {"lat": lat + 1, "lon": lon + 1}
    has_ul = jnp.logical_and(lat > 0, lon > 0)
    has_dr = jnp.logical_and(lat < nlat - 1, lon < nlon - 1)

    barrier = pltpu.get_barrier_semaphore()

    def greet(device):
        pl.semaphore_signal(barrier, inc=1, device_id=device, device_id_type=MESH)

    for side in range(4):
        @pl.when(has[side])
        def _():
            greet(dev[side])

    @pl.when(has_ul)
    def _():
        greet(dev_ul)

    @pl.when(has_dr)
    def _():
        greet(dev_dr)

    def greet_other(k, _):
        t = lax.rem(me + k, n)
        greet({"patch": other, "lat": t // nlon, "lon": lax.rem(t, nlon)})
        return 0

    lax.fori_loop(0, n, greet_other, 0)

    sub = lax.broadcasted_iota(jnp.int32, (1, cbk, lev), 1)
    lane = lax.broadcasted_iota(jnp.int32, (1, cbk, lev), 2)

    def cond(flag, a, b):
        return jnp.where(jnp.full(a.shape, flag.astype(jnp.int32)) == 1, a, b)

    def block(ref, c, rows):
        return ref[pl.ds(c * rows * cbk, rows * cbk), :].reshape(rows, cbk, lev)

    def put(ref, c, rows, value):
        ref[pl.ds(c * rows * cbk, rows * cbk), :] = value.reshape(rows * cbk, lev)

    def pack(k, src, first, count, rows, send_row, send_col):
        for c in range(count):
            o = c * rows * cbk
            f = (first + c)
            send_row[k, 0, pl.ds(f * cbk, cbk), :] = src[pl.ds(o, cbk), :]
            send_row[k, 1, pl.ds(f * cbk, cbk), :] = src[pl.ds(o + (rows - 1) * cbk, cbk), :]
            send_col[k, 0, pl.ds(f * rows, rows), :] = src[pl.ds(o, rows, stride=cbk), :]
            send_col[k, 1, pl.ds(f * rows, rows), :] = src[pl.ds(o + cbk - 1, rows, stride=cbk), :]

    def layer(k, side, count, rows, send_row, recv_row, send_col, recv_col, ss, rs, device):
        back = side ^ 1
        if side < 2:
            m = count * cbk
            return remote(send_row.at[k, back, pl.ds(0, m)], recv_row.at[k, side, pl.ds(0, m)],
                          ss.at[k, back], rs.at[k, side], device)
        m = count * rows
        return remote(send_col.at[k, back - 2, pl.ds(0, m)], recv_col.at[k, side - 2, pl.ds(0, m)],
                      ss.at[k, back], rs.at[k, side], device)

    def start(k, count, rows, *bufs):
        for to in range(4):
            @pl.when(has[to])
            def _():
                layer(k, to ^ 1, count, rows, *bufs, dev[to]).start()

    def arrive(k, count, rows, *bufs):
        for side in range(4):
            @pl.when(has[side])
            def _():
                layer(k, side, count, rows, *bufs, dev[side]).wait_recv()

    def finish(k, count, rows, *bufs):
        for to in range(4):
            @pl.when(has[to])
            def _():
                layer(k, to ^ 1, count, rows, *bufs, dev[to]).wait_send()

    fine = (srow, rrow, scol, rcol, ssem, rsem)
    cvis = (cvs_row, cvr_row, cvs_col, cvr_col, cvssem, cvrsem)
    coarse = (csrow, crrow, cscol, crcol, cssem, crsem)

    pack(0, vel, 0, 3, rb, srow, scol)
    pack(0, visc, 3, 1, rb, srow, scol)
    for c in range(3):
        sdiag[pl.ds(c * cbk, cbk), :] = vel[pl.ds(c * rb * cbk, cbk), :]

    def pair_lane(x):
        return x + jnp.where(lane % 2 == 0, pltpu.roll(x, lev - 1, 2), pltpu.roll(x, 1, 2))

    def pair_sub(x):
        return x + jnp.where(sub % 2 == 0, pltpu.roll(x, cbk - 1, 1), pltpu.roll(x, 1, 1))

    vis = block(visc, 0, rb)
    vis_rows = vis.reshape(hr, 2, cbk, lev)
    vis_rows = vis_rows[:, 0] + vis_rows[:, 1]
    vis_rc = pair_sub(vis_rows)
    vis_rl = pair_lane(vis_rows)
    cvisc = 0.125 * pair_lane(vis_rc)
    put(halo_v, 0, hr, cvisc)
    pack(0, halo_v, 0, 1, hr, cvs_row, cvs_col)

    signals = sum(h.astype(jnp.int32) for h in has) + has_ul.astype(jnp.int32) + has_dr.astype(jnp.int32) + n
    pl.semaphore_wait(barrier, signals)

    start(0, 4, rb, *fine)

    def diagonal_copy(device):
        return remote(sdiag, rdiag, dsem.at[0], dsem.at[1], device)

    @pl.when(has_ul)
    def _():
        diagonal_copy(dev_ul).start()

    start(0, 1, hr, *cvis)

    vr, vc = rb + 1, 2 * cbk
    for c in range(3):
        for r in range(rb):
            view[pl.ds((c * vr + r) * vc, cbk), :] = vel[pl.ds((c * rb + r) * cbk, cbk), :]

    arrive(0, 4, rb, *fine)

    @pl.when(has_dr)
    def _():
        diagonal_copy(dev_dr).wait_recv()

    zero_row = jnp.zeros((cbk, lev), jnp.float32)
    zero_col = jnp.zeros((rb, lev), jnp.float32)
    for c in range(3):
        view[pl.ds((c * vr + rb) * vc, cbk), :] = cond(
            has[1], rrow[0, 1, pl.ds(c * cbk, cbk), :], zero_row)
        view[pl.ds((c * vr + rb) * vc + cbk, cbk), :] = cond(
            has_dr, rdiag[pl.ds(c * cbk, cbk), :], zero_row)
        view[pl.ds(c * vr * vc + cbk, rb, stride=vc), :] = cond(
            has[3], rcol[0, 1, pl.ds(c * rb, rb), :], zero_col)

    for s in range(q):
        base = rows_in[s] * vc + cols_in[s]
        w = [weights[k, s] for k in range(4)]
        for c in range(3):
            o = base + c * vr * vc
            mixed[pl.ds(s * 3 + c, 1), :] = (
                w[0] * view[pl.ds(o, 1), :] + w[1] * view[pl.ds(o + vc, 1), :]
                + w[2] * view[pl.ds(o + 1, 1), :] + w[3] * view[pl.ds(o + vc + 1, 1), :])
    mixed[pl.ds(q * 3, qrows - q * 3), :] = jnp.zeros((qrows - q * 3, lev), jnp.float32)

    def slot_copy(t, source):
        return remote(mixed, gathered.at[pl.ds(pl.multiple_of(source * qrows, 8), qrows)],
                      gsend.at[t], grecv.at[source],
                      {"patch": other, "lat": t // nlon, "lon": lax.rem(t, nlon)})

    def send_slots(k, _):
        slot_copy(lax.rem(me + k, n), me).start()
        return 0

    lax.fori_loop(0, n, send_slots, 0)

    v_up = cond(has[0], rrow[0, 0, pl.ds(3 * cbk, cbk), :], visc[pl.ds(0, cbk), :])
    v_dn = cond(has[1], rrow[0, 1, pl.ds(3 * cbk, cbk), :], visc[pl.ds((rb - 1) * cbk, cbk), :])
    halo[pl.ds(0, rb, stride=cbk), :] = cond(
        has[2], rcol[0, 0, pl.ds(3 * rb, rb), :], scol[0, 0, pl.ds(3 * rb, rb), :])
    halo[pl.ds(cbk - 1, rb, stride=cbk), :] = cond(
        has[3], rcol[0, 1, pl.ds(3 * rb, rb), :], scol[0, 1, pl.ds(3 * rb, rb), :])

    def stack(x, above, below):
        return (jnp.concatenate([above[None], x[:-1]], axis=0),
                jnp.concatenate([x[1:], below[None]], axis=0))

    def beside(x, h):
        return (jnp.where(sub == 0, h, pltpu.roll(x, 1, 1)),
                jnp.where(sub == cbk - 1, h, pltpu.roll(x, cbk - 1, 1)))

    up, dn = stack(vis, v_up, v_dn)
    lf, rt = beside(vis, block(halo, 0, rb))
    bot = jnp.where(lane == 0, vis, pltpu.roll(vis, 1, 2))
    top = jnp.where(lane == lev - 1, vis, pltpu.roll(vis, lev - 1, 2))
    six = [0.5 * (vis + x) for x in (up, dn, lf, rt, bot, top)]
    diag = six[0] + six[1] + six[2] + six[3] + six[4] + six[5]
    inv = 1.0 / diag
    six[4] = jnp.where(lane == 0, 0.0, six[4])
    six[5] = jnp.where(lane == lev - 1, 0.0, six[5])
    for k in range(6):
        put(cf, k, rb, six[k] * inv)
    put(cf, 6, rb, diag)
    for c in range(3):
        put(ff, c, rb, block(force, c, rb) * inv)
        put(v, c, rb, block(vel, c, rb))

    arrive(0, 1, hr, *cvis)
    edge_up = 0.25 * pair_lane(pair_sub(vis[:1]))[0]
    edge_dn = 0.25 * pair_lane(pair_sub(vis[rb - 1:]))[0]
    put(chalo_v, 0, hr, 0.25 * vis_rl)
    edge_lf = chalo_v[pl.ds(0, hr, stride=cbk), :]
    edge_rt = chalo_v[pl.ds(cbk - 1, hr, stride=cbk), :]
    left = cond(has[2], cvr_col[0, 0], edge_lf)
    right = cond(has[3], cvr_col[0, 1], edge_rt)
    for j in range(2):
        chalo[pl.ds(j, hr, stride=cbk), :] = left
        chalo[pl.ds(cbk - 1 - j, hr, stride=cbk), :] = right
    cup, cdn = stack(cvisc, cond(has[0], cvr_row[0, 0], edge_up), cond(has[1], cvr_row[0, 1], edge_dn))

    def beside2(x, h):
        return (jnp.where(sub < 2, h, pltpu.roll(x, 2, 1)),
                jnp.where(sub >= cbk - 2, h, pltpu.roll(x, cbk - 2, 1)))

    clf, crt = beside2(cvisc, block(chalo, 0, hr))
    w = 0.25 * vis_rc
    cbot = jnp.where(lane < 2, jnp.where(lane == 0, w, pltpu.roll(w, 1, 2)), pltpu.roll(cvisc, 2, 2))
    ctop = jnp.where(lane >= lev - 2, jnp.where(lane == lev - 1, w, pltpu.roll(w, lev - 1, 2)),
                     pltpu.roll(cvisc, lev - 2, 2))
    csix = [0.125 * (cvisc + x) for x in (cup, cdn, clf, crt, cbot, ctop)]
    cdiag = csix[0] + csix[1] + csix[2] + csix[3] + csix[4] + csix[5]
    cinv = RELAX / cdiag
    csix[4] = jnp.where(lane < 2, 0.0, csix[4])
    csix[5] = jnp.where(lane >= lev - 2, 0.0, csix[5])
    for k in range(6):
        put(cc, k, hr, csix[k] * cinv)
    put(cc, 6, hr, cinv)

    def slots_arrive(k, _):
        slot_copy(k, k).wait_recv()
        return 0

    lax.fori_loop(0, n, slots_arrive, 0)
    lon_cells = nlon * cbk
    lat_cells = nlat * rb

    def fetch(first, count, out, side):
        for j in range(count):
            s = slots[first + j]
            d = s // q
            base = d * qrows + (s - d * q) * 3
            for c in range(3):
                out[side, pl.ds(c * count + j, 1), :] = gathered[pl.ds(base + c, 1), :]

    for side, first, count, out in (
            (0, lon * cbk, cbk, grow), (1, lon_cells + lon * cbk, cbk, grow),
            (2, 2 * lon_cells + lat * rb, rb, gcol), (3, 2 * lon_cells + lat_cells + lat * rb, rb, gcol)):
        @pl.when(jnp.logical_not(has[side]))
        def _():
            fetch(first, count, out, side % 2)

    parity = lax.rem(lat * rb + lon * cbk, 2) + lax.broadcasted_iota(jnp.int32, (rb, cbk, lev), 0) + sub + lane
    parity = parity % 2

    def halos(k):
        above, below = [], []
        for c in range(3):
            r = pl.ds(c * cbk, cbk)
            above.append(cond(has[0], rrow[k, 0, r, :], grow[0, r, :]))
            below.append(cond(has[1], rrow[k, 1, r, :], grow[1, r, :]))
            m = pl.ds(c * rb, rb)
            o = c * rb * cbk
            halo[pl.ds(o, rb, stride=cbk), :] = cond(has[2], rcol[k, 0, m, :], gcol[0, m, :])
            halo[pl.ds(o + cbk - 1, rb, stride=cbk), :] = cond(has[3], rcol[k, 1, m, :], gcol[1, m, :])
        return above, below

    def jacobi(x, c, above, below, h, coefs, rows, near, step):
        up, dn = stack(x, above, below)
        lf, rt = near(x, h)
        total = block(coefs, 0, rows) * up + block(coefs, 1, rows) * dn
        total = total + block(coefs, 2, rows) * lf + block(coefs, 3, rows) * rt
        total = total + block(coefs, 4, rows) * pltpu.roll(x, step, 2)
        return total + block(coefs, 5, rows) * pltpu.roll(x, lev - step, 2)

    rounds = 2 * SWEEPS
    for k in range(rounds):
        if k > 0:
            arrive(k, 3, rb, *fine)
        above, below = halos(k)
        for c in range(3):
            x = block(v, c, rb)
            relaxed = block(ff, c, rb) + jacobi(x, c, above[c], below[c], block(halo, c, rb), cf, rb, beside, 1)
            put(v, c, rb, jnp.where(parity == k % 2, relaxed, x))
        pack(k + 1, v, 0, 3, rb, srow, scol)
        start(k + 1, 3, rb, *fine)
    arrive(rounds, 3, rb, *fine)
    above, below = halos(rounds)
    for c in range(3):
        x = block(v, c, rb)
        relaxed = block(ff, c, rb) + jacobi(x, c, above[c], below[c], block(halo, c, rb), cf, rb, beside, 1)
        residual = block(cf, 6, rb) * (relaxed - x)
        put(res_out, c, rb, residual)
        pairs = residual.reshape(hr, 2, cbk, lev)
        rhs = 0.125 * pair_lane(pair_sub(pairs[:, 0] + pairs[:, 1]))
        e = rhs * block(cc, 6, hr)
        put(cb, c, hr, e)
        put(ce, c, hr, e)

    zero = jnp.zeros((cbk, lev), jnp.float32)
    zeros = jnp.zeros((hr, lev), jnp.float32)
    for k in range(COARSE - 1):
        pack(k, ce, 0, 3, hr, csrow, cscol)
        start(k, 3, hr, *coarse)
        arrive(k, 3, hr, *coarse)
        for c in range(3):
            r = pl.ds(c * cbk, cbk)
            m = pl.ds(c * hr, hr)
            o = c * hr * cbk
            left = cond(has[2], crcol[k, 0, m, :], zeros)
            right = cond(has[3], crcol[k, 1, m, :], zeros)
            for j in range(2):
                chalo[pl.ds(o + j, hr, stride=cbk), :] = left
                chalo[pl.ds(o + cbk - 1 - j, hr, stride=cbk), :] = right
            x = block(ce, c, hr)
            put(ce, c, hr, block(cb, c, hr) + (1.0 - RELAX) * x + jacobi(
                x, c, cond(has[0], crrow[k, 0, r, :], zero), cond(has[1], crrow[k, 1, r, :], zero),
                block(chalo, c, hr), cc, hr, beside2, 2))

    for c in range(3):
        e = block(ce, c, hr)
        e = jnp.broadcast_to(e[:, None], (hr, 2, cbk, lev)).reshape(rb, cbk, lev)
        put(new_out, c, rb, block(v, c, rb) + e)

    finish(0, 4, rb, *fine)
    for k in range(rounds):
        finish(k + 1, 3, rb, *fine)
    finish(0, 1, hr, *cvis)
    for k in range(COARSE - 1):
        finish(k, 3, hr, *coarse)

    @pl.when(has_ul)
    def _():
        diagonal_copy(dev_ul).wait_send()

    def slots_sent(k, _):
        slot_copy(k, me).wait_send()
        return 0

    lax.fori_loop(0, n, slots_sent, 0)


def per_device(velocity, forcing, viscosity, ghost_slots, corner_rows, corner_cols, corner_weights):
    _, _, rb, cbk, lev = velocity.shape
    nlat, nlon = lax.axis_size("lat"), lax.axis_size("lon")
    n = nlat * nlon
    q = corner_rows.shape[-1]
    qrows = -(-3 * q // 8) * 8 + (8 if (3 * q) % 8 == 0 else 0)
    hr = rb // 2
    flat = rb * cbk
    rounds = 2 * SWEEPS + 1
    f32 = jnp.float32
    vm = lambda *shape: pltpu.VMEM(shape, f32)
    dma = lambda *shape: pltpu.SemaphoreType.DMA(shape)
    vspec = pl.BlockSpec(memory_space=pltpu.VMEM)
    sspec = pl.BlockSpec(memory_space=pltpu.SMEM)
    ck = COARSE - 1
    new, res = pl.pallas_call(
        functools.partial(kernel, (rb, cbk, lev, nlat, nlon, q, qrows)),
        out_shape=[jax.ShapeDtypeStruct((3 * flat, lev), f32)] * 2,
        in_specs=[vspec] * 3 + [sspec] * 4,
        out_specs=[vspec] * 2,
        scratch_shapes=[
            vm(3 * flat, lev), vm(3 * flat, lev), vm(7 * flat, lev), vm(3 * flat, lev), vm(flat, lev),
            vm(rounds, 2, 4 * cbk, lev), vm(rounds, 2, 4 * cbk, lev),
            vm(rounds, 2, 4 * rb, lev), vm(rounds, 2, 4 * rb, lev),
            dma(rounds, 4), dma(rounds, 4),
            vm(3 * cbk, lev), vm(3 * cbk, lev), dma(2),
            vm(3 * (rb + 1) * 2 * cbk, lev), vm(qrows, lev), vm(n * qrows, lev), dma(n), dma(n),
            vm(2, 3 * cbk, lev), vm(2, 3 * rb, lev),
            vm(1, 2, cbk, lev), vm(1, 2, cbk, lev), vm(1, 2, hr, lev), vm(1, 2, hr, lev), dma(1, 4), dma(1, 4),
            vm(3 * hr * cbk, lev), vm(3 * hr * cbk, lev), vm(7 * hr * cbk, lev), vm(3 * hr * cbk, lev), vm(hr * cbk, lev),
            vm(ck, 2, 3 * cbk, lev), vm(ck, 2, 3 * cbk, lev), vm(ck, 2, 3 * hr, lev), vm(ck, 2, 3 * hr, lev),
            dma(ck, 4), dma(ck, 4),
        ],
        compiler_params=pltpu.CompilerParams(
            collective_id=0, has_side_effects=True, vmem_limit_bytes=32 * 2**20),
    )(velocity.reshape(3 * flat, lev), forcing.reshape(3 * flat, lev), viscosity.reshape(flat, lev),
      ghost_slots[0], corner_rows.reshape(q), corner_cols.reshape(q), corner_weights.reshape(4, q))
    return new.reshape(velocity.shape), res.reshape(velocity.shape)


def solution(mesh):
    placed = (
        P("patch", None, "lat", "lon", None),
        P("patch", None, "lat", "lon", None),
        P("patch", "lat", "lon", None),
        P("patch", None),
        P("patch", "lat", "lon"),
        P("patch", "lat", "lon"),
        P("patch", "lat", None, "lon"),
    )
    return jax.shard_map(
        per_device,
        mesh=mesh,
        in_specs=placed,
        out_specs=(P("patch", None, "lat", "lon", None), P("patch", None, "lat", "lon", None)),
        check_vma=False,
    )
```

```python
import functools
import jax
import jax.numpy as jnp
from jax import lax
from jax.experimental import pallas as pl
from jax.experimental.pallas import tpu as pltpu
from jax.sharding import PartitionSpec as P

SWEEPS = 2
COARSE = 8
RELAX = 0.8
MESH = pl.DeviceIdType.MESH


def box_reach(hr, cw):
    return -(-COARSE // hr), -(-COARSE // cw)


def remote(src, dst, send_sem, recv_sem, device):
    return pltpu.make_async_remote_copy(
        src_ref=src, dst_ref=dst, send_sem=send_sem, recv_sem=recv_sem,
        device_id=device, device_id_type=MESH)


def kernel(sizes, vel, force, visc, slots, rows_in, cols_in, weights, new_out, res_out,
           v, ff, cf, halo, halo_v, srow, rrow, scol, rcol, ssem, rsem,
           sdiag, rdiag, dsem, view, mixed, gathered, gsend, grecv, grow, gcol,
           vbox, vbsend, vbrecv, rbox, rbsend, rbrecv, ce, chalo_v, cvreg, cc, rhs_reg, err_reg):
    rb, cbk, lev, nlat, nlon, q, qrows = sizes
    hr = rb // 2
    cw = cbk // 2
    near_lat, near_lon = box_reach(hr, cw)
    wide = 2 * near_lon + 1
    n = nlat * nlon
    lat = lax.axis_index("lat")
    lon = lax.axis_index("lon")
    patch = lax.axis_index("patch")
    other = 1 - patch
    me = lat * nlon + lon
    has = (lat > 0, lat < nlat - 1, lon > 0, lon < nlon - 1)
    dev = ({"lat": lat - 1}, {"lat": lat + 1}, {"lon": lon - 1}, {"lon": lon + 1})
    dev_ul = {"lat": lat - 1, "lon": lon - 1}
    dev_dr = {"lat": lat + 1, "lon": lon + 1}
    has_ul = jnp.logical_and(lat > 0, lon > 0)
    has_dr = jnp.logical_and(lat < nlat - 1, lon < nlon - 1)

    barrier = pltpu.get_barrier_semaphore()

    def greet(device):
        pl.semaphore_signal(barrier, inc=1, device_id=device, device_id_type=MESH)

    offsets = [(dl, dc) for dl in range(-near_lat, near_lat + 1) for dc in range(-near_lon, near_lon + 1)
               if (dl, dc) != (0, 0)]
    offsets.sort(key=lambda o: -abs(o[0]) - abs(o[1]))

    def exists(dl, dc):
        return ((lat + dl >= 0) & (lat + dl < nlat)) & ((lon + dc >= 0) & (lon + dc < nlon))

    def box_index(dl, dc):
        return (dl + near_lat) * wide + dc + near_lon

    home = box_index(0, 0)
    around = [exists(dl, dc) for dl, dc in offsets]
    for (dl, dc), there in zip(offsets, around):
        @pl.when(there)
        def _():
            greet({"lat": lat + dl, "lon": lon + dc})

    def box_copy(buf, send, recv, dl, dc, target):
        at = box_index(-dl, -dc)
        return remote(buf.at[home], buf.at[at], send.at[at], recv.at[at], target)

    def box_start(*bufs):
        for (dl, dc), there in zip(offsets, around):
            @pl.when(there)
            def _():
                box_copy(*bufs, dl, dc, {"lat": lat + dl, "lon": lon + dc}).start()

    def box_arrive(*bufs):
        for (dl, dc), there in zip(offsets, around):
            @pl.when(there)
            def _():
                box_copy(*bufs, -dl, -dc, {"lat": lat + dl, "lon": lon + dc}).wait_recv()

    def box_finish(*bufs):
        for (dl, dc), there in zip(offsets, around):
            @pl.when(there)
            def _():
                box_copy(*bufs, dl, dc, {"lat": lat + dl, "lon": lon + dc}).wait_send()

    def greet_other(k, _):
        t = lax.rem(me + k, n)
        greet({"patch": other, "lat": t // nlon, "lon": lax.rem(t, nlon)})
        return 0

    lax.fori_loop(0, n, greet_other, 0)

    sub = lax.broadcasted_iota(jnp.int32, (1, cbk, lev), 1)
    lane = lax.broadcasted_iota(jnp.int32, (1, cbk, lev), 2)

    def cond(flag, a, b):
        return jnp.where(jnp.full(a.shape, flag.astype(jnp.int32)) == 1, a, b)

    def block(ref, c, rows):
        return ref[pl.ds(c * rows * cbk, rows * cbk), :].reshape(rows, cbk, lev)

    def put(ref, c, rows, value):
        ref[pl.ds(c * rows * cbk, rows * cbk), :] = value.reshape(rows * cbk, lev)

    def pack(k, src, first, count, rows, send_row, send_col):
        for c in range(count):
            o = c * rows * cbk
            f = (first + c)
            send_row[k, 0, pl.ds(f * cbk, cbk), :] = src[pl.ds(o, cbk), :]
            send_row[k, 1, pl.ds(f * cbk, cbk), :] = src[pl.ds(o + (rows - 1) * cbk, cbk), :]
            send_col[k, 0, pl.ds(f * rows, rows), :] = src[pl.ds(o, rows, stride=cbk), :]
            send_col[k, 1, pl.ds(f * rows, rows), :] = src[pl.ds(o + cbk - 1, rows, stride=cbk), :]

    def layer(k, side, count, rows, send_row, recv_row, send_col, recv_col, ss, rs, device):
        back = side ^ 1
        if side < 2:
            m = count * cbk
            return remote(send_row.at[k, back, pl.ds(0, m)], recv_row.at[k, side, pl.ds(0, m)],
                          ss.at[k, back], rs.at[k, side], device)
        m = count * rows
        return remote(send_col.at[k, back - 2, pl.ds(0, m)], recv_col.at[k, side - 2, pl.ds(0, m)],
                      ss.at[k, back], rs.at[k, side], device)

    def start(k, count, rows, *bufs):
        for to in range(4):
            @pl.when(has[to])
            def _():
                layer(k, to ^ 1, count, rows, *bufs, dev[to]).start()

    def arrive(k, count, rows, *bufs):
        for side in range(4):
            @pl.when(has[side])
            def _():
                layer(k, side, count, rows, *bufs, dev[side]).wait_recv()

    def finish(k, count, rows, *bufs):
        for to in range(4):
            @pl.when(has[to])
            def _():
                layer(k, to ^ 1, count, rows, *bufs, dev[to]).wait_send()

    fine = (srow, rrow, scol, rcol, ssem, rsem)
    cvis = (vbox, vbsend, vbrecv)
    coarse = (rbox, rbsend, rbrecv)

    pack(0, vel, 0, 3, rb, srow, scol)
    pack(0, visc, 3, 1, rb, srow, scol)
    for c in range(3):
        sdiag[pl.ds(c * cbk, cbk), :] = vel[pl.ds(c * rb * cbk, cbk), :]

    def pair_lane(x):
        return x + jnp.where(lane % 2 == 0, pltpu.roll(x, lev - 1, 2), pltpu.roll(x, 1, 2))

    def pair_sub(x):
        return x + jnp.where(sub % 2 == 0, pltpu.roll(x, cbk - 1, 1), pltpu.roll(x, 1, 1))

    vis = block(visc, 0, rb)
    vis_rows = vis.reshape(hr, 2, cbk, lev)
    vis_rows = vis_rows[:, 0] + vis_rows[:, 1]
    vis_rc = pair_sub(vis_rows)
    vis_rl = pair_lane(vis_rows)
    cvisc = 0.125 * pair_lane(vis_rc)
    ends = 0.25 * vis_rc
    marked = jnp.where(lane == 1, pltpu.roll(ends, 1, 2),
                       jnp.where(lane == lev - 2, pltpu.roll(ends, lev - 1, 2), cvisc))
    put(halo_v, 0, hr, marked)
    put(chalo_v, 0, hr, 0.25 * vis_rl)
    for j in range(cw):
        vbox[home, pl.ds(j * hr, hr), :] = halo_v[pl.ds(2 * j, hr, stride=cbk), :]
    vbox[home, pl.ds((cw + 1) * hr, hr), :] = cond(
        has[2], chalo_v[pl.ds(cbk - 1, hr, stride=cbk), :], chalo_v[pl.ds(0, hr, stride=cbk), :])
    edge = cond(has[0], 0.25 * pair_lane(pair_sub(vis[rb - 1:]))[0], 0.25 * pair_lane(pair_sub(vis[:1]))[0])
    vbox[home, pl.ds(cw * hr, cbk), :] = edge
    cvreg[...] = jnp.ones(cvreg.shape, jnp.float32)
    for (dl, dc), there in zip(offsets, around):
        @pl.when(jnp.logical_not(there))
        def _():
            rbox[box_index(dl, dc)] = jnp.zeros(rbox.shape[1:], jnp.float32)

    signals = sum(there.astype(jnp.int32) for there in around) + n
    pl.semaphore_wait(barrier, signals)

    start(0, 4, rb, *fine)

    def diagonal_copy(device):
        return remote(sdiag, rdiag, dsem.at[0], dsem.at[1], device)

    @pl.when(has_ul)
    def _():
        diagonal_copy(dev_ul).start()


    vr, vc = rb + 1, 2 * cbk
    for c in range(3):
        for r in range(rb):
            view[pl.ds((c * vr + r) * vc, cbk), :] = vel[pl.ds((c * rb + r) * cbk, cbk), :]

    arrive(0, 4, rb, *fine)

    @pl.when(has_dr)
    def _():
        diagonal_copy(dev_dr).wait_recv()

    zero_row = jnp.zeros((cbk, lev), jnp.float32)
    zero_col = jnp.zeros((rb, lev), jnp.float32)
    for c in range(3):
        view[pl.ds((c * vr + rb) * vc, cbk), :] = cond(
            has[1], rrow[0, 1, pl.ds(c * cbk, cbk), :], zero_row)
        view[pl.ds((c * vr + rb) * vc + cbk, cbk), :] = cond(
            has_dr, rdiag[pl.ds(c * cbk, cbk), :], zero_row)
        view[pl.ds(c * vr * vc + cbk, rb, stride=vc), :] = cond(
            has[3], rcol[0, 1, pl.ds(c * rb, rb), :], zero_col)

    for s in range(q):
        base = rows_in[s] * vc + cols_in[s]
        w = [weights[k, s] for k in range(4)]
        for c in range(3):
            o = base + c * vr * vc
            mixed[pl.ds(s * 3 + c, 1), :] = (
                w[0] * view[pl.ds(o, 1), :] + w[1] * view[pl.ds(o + vc, 1), :]
                + w[2] * view[pl.ds(o + 1, 1), :] + w[3] * view[pl.ds(o + vc + 1, 1), :])
    mixed[pl.ds(q * 3, qrows - q * 3), :] = jnp.zeros((qrows - q * 3, lev), jnp.float32)

    def slot_copy(t, source):
        return remote(mixed, gathered.at[pl.ds(pl.multiple_of(source * qrows, 8), qrows)],
                      gsend.at[t], grecv.at[source],
                      {"patch": other, "lat": t // nlon, "lon": lax.rem(t, nlon)})

    def send_slots(k, _):
        slot_copy(lax.rem(me + k, n), me).start()
        return 0

    lax.fori_loop(0, n, send_slots, 0)
    box_start(*cvis)

    v_up = cond(has[0], rrow[0, 0, pl.ds(3 * cbk, cbk), :], visc[pl.ds(0, cbk), :])
    v_dn = cond(has[1], rrow[0, 1, pl.ds(3 * cbk, cbk), :], visc[pl.ds((rb - 1) * cbk, cbk), :])
    halo[pl.ds(0, rb, stride=cbk), :] = cond(
        has[2], rcol[0, 0, pl.ds(3 * rb, rb), :], scol[0, 0, pl.ds(3 * rb, rb), :])
    halo[pl.ds(cbk - 1, rb, stride=cbk), :] = cond(
        has[3], rcol[0, 1, pl.ds(3 * rb, rb), :], scol[0, 1, pl.ds(3 * rb, rb), :])

    def stack(x, above, below):
        return (jnp.concatenate([above[None], x[:-1]], axis=0),
                jnp.concatenate([x[1:], below[None]], axis=0))

    def beside(x, h):
        return (jnp.where(sub == 0, h, pltpu.roll(x, 1, 1)),
                jnp.where(sub == cbk - 1, h, pltpu.roll(x, cbk - 1, 1)))

    up, dn = stack(vis, v_up, v_dn)
    lf, rt = beside(vis, block(halo, 0, rb))
    bot = jnp.where(lane == 0, vis, pltpu.roll(vis, 1, 2))
    top = jnp.where(lane == lev - 1, vis, pltpu.roll(vis, lev - 1, 2))
    six = [0.5 * (vis + x) for x in (up, dn, lf, rt, bot, top)]
    diag = six[0] + six[1] + six[2] + six[3] + six[4] + six[5]
    inv = 1.0 / diag
    six[4] = jnp.where(lane == 0, 0.0, six[4])
    six[5] = jnp.where(lane == lev - 1, 0.0, six[5])
    for k in range(6):
        put(cf, k, rb, six[k] * inv)
    put(cf, 6, rb, diag)
    for c in range(3):
        put(ff, c, rb, block(force, c, rb) * inv)
        put(v, c, rb, block(vel, c, rb))

    box_arrive(*cvis)
    cols, rows_r = cvreg.shape[0], cvreg.shape[1]
    first_col, first_row = near_lon * cw, near_lat * hr

    for dl, dc in offsets + [(0, 0)]:
        @pl.when(exists(dl, dc))
        def _():
            for j in range(cw):
                cvreg[(dc + near_lon) * cw + j, pl.ds((dl + near_lat) * hr, hr), :] = (
                    vbox[box_index(dl, dc), pl.ds(j * hr, hr), :])
    for dc in range(-near_lon, near_lon + 1):
        for at_edge, row in ((lat == 0, first_row - 1), (lat == nlat - 1, first_row + hr)):
            @pl.when(at_edge & exists(0, dc))
            def _():
                for j in range(cw):
                    cvreg[(dc + near_lon) * cw + j, pl.ds(row, 1), :] = (
                        vbox[box_index(0, dc), pl.ds(cw * hr + 2 * j, 1), :])
    for dc in range(-near_lon, near_lon + 1):
        for at_edge, col in ((lon + dc == 0, (dc + near_lon) * cw - 1),
                             (lon + dc == nlon - 1, (dc + near_lon + 1) * cw)):
            if 0 <= col < cols:
                for dl in range(-near_lat, near_lat + 1):
                    @pl.when(at_edge & exists(dl, dc))
                    def _():
                        cvreg[col, pl.ds((dl + near_lat) * hr, hr), :] = (
                            vbox[box_index(dl, dc), pl.ds((cw + 1) * hr, hr), :])
    lane_r = lax.broadcasted_iota(jnp.int32, (1, rows_r, lev), 2)
    row_r = lat * hr - first_row + lax.broadcasted_iota(jnp.int32, (1, rows_r, lev), 1)
    rows_ok = (row_r >= 0) & (row_r < nlat * hr)

    def whole(x):
        return jnp.where(lane_r == 1, pltpu.roll(x, 1, 2),
                         jnp.where(lane_r == lev - 2, pltpu.roll(x, lev - 1, 2), x))

    for col in range(1, cols - 1):
        m = cvreg[pl.ds(col, 1)]
        mid = whole(m)
        cbot = jnp.where(lane_r == 0, pltpu.roll(m, lev - 1, 2), jnp.where(lane_r == 1, m, pltpu.roll(mid, 2, 2)))
        ctop = jnp.where(lane_r == lev - 1, pltpu.roll(m, 1, 2),
                         jnp.where(lane_r == lev - 2, m, pltpu.roll(mid, lev - 2, 2)))
        csix = [0.125 * (mid + x) for x in (
            pltpu.roll(mid, 1, 1), pltpu.roll(mid, rows_r - 1, 1),
            whole(cvreg[pl.ds(col - 1, 1)]), whole(cvreg[pl.ds(col + 1, 1)]), cbot, ctop)]
        cdiag = csix[0] + csix[1] + csix[2] + csix[3] + csix[4] + csix[5]
        col_g = lon * cw - first_col + col
        inside = ((col_g >= 0) & (col_g < nlon * cw)).astype(jnp.int32)
        keep = rows_ok & (jnp.full(rows_ok.shape, inside) == 1)
        cinv = jnp.where(keep, RELAX / cdiag, 0.0)
        csix[4] = jnp.where(lane_r < 2, 0.0, csix[4])
        csix[5] = jnp.where(lane_r >= lev - 2, 0.0, csix[5])
        for k in range(6):
            cc[k, pl.ds(col, 1)] = csix[k] * cinv
        cc[6, pl.ds(col, 1)] = cinv

    def slots_arrive(k, _):
        slot_copy(k, k).wait_recv()
        return 0

    lax.fori_loop(0, n, slots_arrive, 0)
    lon_cells = nlon * cbk
    lat_cells = nlat * rb

    def fetch(first, count, out, side):
        for j in range(count):
            s = slots[first + j]
            d = s // q
            base = d * qrows + (s - d * q) * 3
            for c in range(3):
                out[side, pl.ds(c * count + j, 1), :] = gathered[pl.ds(base + c, 1), :]

    for side, first, count, out in (
            (0, lon * cbk, cbk, grow), (1, lon_cells + lon * cbk, cbk, grow),
            (2, 2 * lon_cells + lat * rb, rb, gcol), (3, 2 * lon_cells + lat_cells + lat * rb, rb, gcol)):
        @pl.when(jnp.logical_not(has[side]))
        def _():
            fetch(first, count, out, side % 2)

    parity = lax.rem(lat * rb + lon * cbk, 2) + lax.broadcasted_iota(jnp.int32, (rb, cbk, lev), 0) + sub + lane
    parity = parity % 2

    def halos(k):
        above, below = [], []
        for c in range(3):
            r = pl.ds(c * cbk, cbk)
            above.append(cond(has[0], rrow[k, 0, r, :], grow[0, r, :]))
            below.append(cond(has[1], rrow[k, 1, r, :], grow[1, r, :]))
            m = pl.ds(c * rb, rb)
            o = c * rb * cbk
            halo[pl.ds(o, rb, stride=cbk), :] = cond(has[2], rcol[k, 0, m, :], gcol[0, m, :])
            halo[pl.ds(o + cbk - 1, rb, stride=cbk), :] = cond(has[3], rcol[k, 1, m, :], gcol[1, m, :])
        return above, below

    def jacobi(x, c, above, below, h, coefs, rows, near, step):
        up, dn = stack(x, above, below)
        lf, rt = near(x, h)
        total = block(coefs, 0, rows) * up + block(coefs, 1, rows) * dn
        total = total + block(coefs, 2, rows) * lf + block(coefs, 3, rows) * rt
        total = total + block(coefs, 4, rows) * pltpu.roll(x, step, 2)
        return total + block(coefs, 5, rows) * pltpu.roll(x, lev - step, 2)

    rounds = 2 * SWEEPS
    for k in range(rounds):
        if k > 0:
            arrive(k, 3, rb, *fine)
        above, below = halos(k)
        for c in range(3):
            x = block(v, c, rb)
            relaxed = block(ff, c, rb) + jacobi(x, c, above[c], below[c], block(halo, c, rb), cf, rb, beside, 1)
            put(v, c, rb, jnp.where(parity == k % 2, relaxed, x))
        pack(k + 1, v, 0, 3, rb, srow, scol)
        start(k + 1, 3, rb, *fine)
    arrive(rounds, 3, rb, *fine)
    above, below = halos(rounds)
    for c in range(3):
        x = block(v, c, rb)
        relaxed = block(ff, c, rb) + jacobi(x, c, above[c], below[c], block(halo, c, rb), cf, rb, beside, 1)
        residual = block(cf, 6, rb) * (relaxed - x)
        put(res_out, c, rb, residual)
        pairs = residual.reshape(hr, 2, cbk, lev)
        rhs = 0.125 * pair_lane(pair_sub(pairs[:, 0] + pairs[:, 1]))
        put(ce, c, hr, rhs)
        for j in range(cw // 2):
            first = ce[pl.ds(c * hr * cbk + 2 * j, hr, stride=cbk), :]
            second = ce[pl.ds(c * hr * cbk + 2 * (j + cw // 2), hr, stride=cbk), :]
            rbox[home, pl.ds((c * (cw // 2) + j) * hr, hr), :] = jnp.where(lane[0] % 2 == 0, first, second)
    box_start(*coarse)
    box_arrive(*coarse)
    for dl in range(-near_lat, near_lat + 1):
        for dc in range(-near_lon, near_lon + 1):
            r = pl.ds((dl + near_lat) * hr, hr)
            for c in range(3):
                for j in range(cw // 2):
                    both = rbox[box_index(dl, dc), pl.ds((c * (cw // 2) + j) * hr, hr), :]
                    col = (dc + near_lon) * cw + j
                    rhs_reg[c, col, r, :] = jnp.where(lane[0] % 2 == 0, both, pltpu.roll(both, 1, 1))
                    rhs_reg[c, col + cw // 2, r, :] = jnp.where(lane[0] % 2 == 0, pltpu.roll(both, lev - 1, 1), both)
    for c in range(3):
        for col in range(1, cols - 1):
            e = rhs_reg[c, col] * cc[6, col]
            rhs_reg[c, col] = e
            err_reg[c, col] = e
    for k in range(COARSE - 1):
        depth = COARSE - 2 - k
        lo, hi = first_col - depth, first_col + cw + depth
        for c in range(3):
            x = err_reg[c, pl.ds(lo - 1, hi - lo + 2)]
            mid = x[1:-1]
            w = pl.ds(lo, hi - lo)
            total = rhs_reg[c, w] + (1.0 - RELAX) * mid
            total = total + cc[0, w] * pltpu.roll(mid, 1, 1) + cc[1, w] * pltpu.roll(mid, rows_r - 1, 1)
            total = total + cc[2, w] * x[:-2] + cc[3, w] * x[2:]
            total = total + cc[4, w] * pltpu.roll(mid, 2, 2) + cc[5, w] * pltpu.roll(mid, lev - 2, 2)
            err_reg[c, w] = total
    for c in range(3):
        for j in range(cw):
            tile = err_reg[c, first_col + j, pl.ds(first_row, hr), :]
            for twin in range(2):
                ce[pl.ds(c * hr * cbk + 2 * j + twin, hr, stride=cbk), :] = tile

    for c in range(3):
        e = block(ce, c, hr)
        e = jnp.broadcast_to(e[:, None], (hr, 2, cbk, lev)).reshape(rb, cbk, lev)
        put(new_out, c, rb, block(v, c, rb) + e)

    finish(0, 4, rb, *fine)
    for k in range(rounds):
        finish(k + 1, 3, rb, *fine)
    box_finish(*cvis)
    box_finish(*coarse)

    @pl.when(has_ul)
    def _():
        diagonal_copy(dev_ul).wait_send()

    def slots_sent(k, _):
        slot_copy(k, me).wait_send()
        return 0

    lax.fori_loop(0, n, slots_sent, 0)


def per_device(velocity, forcing, viscosity, ghost_slots, corner_rows, corner_cols, corner_weights):
    _, _, rb, cbk, lev = velocity.shape
    nlat, nlon = lax.axis_size("lat"), lax.axis_size("lon")
    n = nlat * nlon
    q = corner_rows.shape[-1]
    qrows = -(-3 * q // 8) * 8 + (8 if (3 * q) % 8 == 0 else 0)
    hr = rb // 2
    flat = rb * cbk
    rounds = 2 * SWEEPS + 1
    f32 = jnp.float32
    vm = lambda *shape: pltpu.VMEM(shape, f32)
    dma = lambda *shape: pltpu.SemaphoreType.DMA(shape)
    vspec = pl.BlockSpec(memory_space=pltpu.VMEM)
    sspec = pl.BlockSpec(memory_space=pltpu.SMEM)
    cw = cbk // 2
    near_lat, near_lon = box_reach(hr, cw)
    nbox = (2 * near_lat + 1) * (2 * near_lon + 1)
    cols, rows_r = (2 * near_lon + 1) * cw, (2 * near_lat + 1) * hr
    new, res = pl.pallas_call(
        functools.partial(kernel, (rb, cbk, lev, nlat, nlon, q, qrows)),
        out_shape=[jax.ShapeDtypeStruct((3 * flat, lev), f32)] * 2,
        in_specs=[vspec] * 3 + [sspec] * 4,
        out_specs=[vspec] * 2,
        scratch_shapes=[
            vm(3 * flat, lev), vm(3 * flat, lev), vm(7 * flat, lev), vm(3 * flat, lev), vm(flat, lev),
            vm(rounds, 2, 4 * cbk, lev), vm(rounds, 2, 4 * cbk, lev),
            vm(rounds, 2, 4 * rb, lev), vm(rounds, 2, 4 * rb, lev),
            dma(rounds, 4), dma(rounds, 4),
            vm(3 * cbk, lev), vm(3 * cbk, lev), dma(2),
            vm(3 * (rb + 1) * 2 * cbk, lev), vm(qrows, lev), vm(n * qrows, lev), dma(n), dma(n),
            vm(2, 3 * cbk, lev), vm(2, 3 * rb, lev),
            vm(nbox, (cw + 2) * hr, lev), dma(nbox), dma(nbox), vm(nbox, 3 * cw // 2 * hr, lev), dma(nbox), dma(nbox),
            vm(3 * hr * cbk, lev), vm(hr * cbk, lev), vm(cols, rows_r, lev), vm(7, cols, rows_r, lev),
            vm(3, cols, rows_r, lev), vm(3, cols, rows_r, lev),
        ],
        compiler_params=pltpu.CompilerParams(
            collective_id=0, has_side_effects=True, vmem_limit_bytes=32 * 2**20),
    )(velocity.reshape(3 * flat, lev), forcing.reshape(3 * flat, lev), viscosity.reshape(flat, lev),
      ghost_slots[0], corner_rows.reshape(q), corner_cols.reshape(q), corner_weights.reshape(4, q))
    return new.reshape(velocity.shape), res.reshape(velocity.shape)


def solution(mesh):
    placed = (
        P("patch", None, "lat", "lon", None),
        P("patch", None, "lat", "lon", None),
        P("patch", "lat", "lon", None),
        P("patch", None),
        P("patch", "lat", "lon"),
        P("patch", "lat", "lon"),
        P("patch", "lat", None, "lon"),
    )
    return jax.shard_map(
        per_device,
        mesh=mesh,
        in_specs=placed,
        out_specs=(P("patch", None, "lat", "lon", None), P("patch", None, "lat", "lon", None)),
        check_vma=False,
    )
```

```python
import functools
import jax
import jax.numpy as jnp
from jax import lax
from jax.experimental import pallas as pl
from jax.experimental.pallas import tpu as pltpu
from jax.sharding import PartitionSpec as P

SWEEPS = 2
COARSE = 8
RELAX = 0.8
MESH = pl.DeviceIdType.MESH


def box_reach(hr, cw):
    return -(-COARSE // hr), -(-COARSE // cw)


def remote(src, dst, send_sem, recv_sem, device):
    return pltpu.make_async_remote_copy(
        src_ref=src, dst_ref=dst, send_sem=send_sem, recv_sem=recv_sem,
        device_id=device, device_id_type=MESH)


def kernel(sizes, vel, force, visc, slots, rows_in, cols_in, weights, new_out, res_out,
           v, ff, cf, halo, halo_v, srow, rrow, scol, rcol, ssem, rsem,
           sdiag, rdiag, dsem, view, mixed, gathered, gsend, grecv, grow, gcol,
           vbox, vbsend, vbrecv, rbox, rbsend, rbrecv, ce, chalo_v, cvreg, cc, rhs_reg, err_reg):
    rb, cbk, lev, nlat, nlon, q, qrows = sizes
    hr = rb // 2
    cw = cbk // 2
    near_lat, near_lon = box_reach(hr, cw)
    wide = 2 * near_lon + 1
    n = nlat * nlon
    lat = lax.axis_index("lat")
    lon = lax.axis_index("lon")
    patch = lax.axis_index("patch")
    other = 1 - patch
    me = lat * nlon + lon
    has = (lat > 0, lat < nlat - 1, lon > 0, lon < nlon - 1)
    dev = ({"lat": lat - 1}, {"lat": lat + 1}, {"lon": lon - 1}, {"lon": lon + 1})
    dev_ul = {"lat": lat - 1, "lon": lon - 1}
    dev_dr = {"lat": lat + 1, "lon": lon + 1}
    has_ul = jnp.logical_and(lat > 0, lon > 0)
    has_dr = jnp.logical_and(lat < nlat - 1, lon < nlon - 1)

    barrier = pltpu.get_barrier_semaphore()

    def greet(device):
        pl.semaphore_signal(barrier, inc=1, device_id=device, device_id_type=MESH)

    offsets = [(dl, dc) for dl in range(-near_lat, near_lat + 1) for dc in range(-near_lon, near_lon + 1)
               if (dl, dc) != (0, 0)]
    offsets.sort(key=lambda o: -abs(o[0]) - abs(o[1]))

    def exists(dl, dc):
        return ((lat + dl >= 0) & (lat + dl < nlat)) & ((lon + dc >= 0) & (lon + dc < nlon))

    def box_index(dl, dc):
        return (dl + near_lat) * wide + dc + near_lon

    home = box_index(0, 0)
    around = [exists(dl, dc) for dl, dc in offsets]
    for (dl, dc), there in zip(offsets, around):
        @pl.when(there)
        def _():
            greet({"lat": lat + dl, "lon": lon + dc})

    def box_copy(buf, send, recv, dl, dc, target):
        at = box_index(-dl, -dc)
        return remote(buf.at[home], buf.at[at], send.at[at], recv.at[at], target)

    def box_start(*bufs):
        for (dl, dc), there in zip(offsets, around):
            @pl.when(there)
            def _():
                box_copy(*bufs, dl, dc, {"lat": lat + dl, "lon": lon + dc}).start()

    def box_arrive(*bufs):
        for (dl, dc), there in zip(offsets, around):
            @pl.when(there)
            def _():
                box_copy(*bufs, -dl, -dc, {"lat": lat + dl, "lon": lon + dc}).wait_recv()

    def box_finish(*bufs):
        for (dl, dc), there in zip(offsets, around):
            @pl.when(there)
            def _():
                box_copy(*bufs, dl, dc, {"lat": lat + dl, "lon": lon + dc}).wait_send()

    def greet_other(k, _):
        t = lax.rem(me + k, n)
        greet({"patch": other, "lat": t // nlon, "lon": lax.rem(t, nlon)})
        return 0

    lax.fori_loop(0, n, greet_other, 0)

    sub = lax.broadcasted_iota(jnp.int32, (1, cbk, lev), 1)
    lane = lax.broadcasted_iota(jnp.int32, (1, cbk, lev), 2)

    def cond(flag, a, b):
        return jnp.where(jnp.full(a.shape, flag.astype(jnp.int32)) == 1, a, b)

    def block(ref, c, rows):
        return ref[pl.ds(c * rows * cbk, rows * cbk), :].reshape(rows, cbk, lev)

    def put(ref, c, rows, value):
        ref[pl.ds(c * rows * cbk, rows * cbk), :] = value.reshape(rows * cbk, lev)

    def pack(k, src, first, count, rows, send_row, send_col):
        for c in range(count):
            o = c * rows * cbk
            f = (first + c)
            send_row[k, 0, pl.ds(f * cbk, cbk), :] = src[pl.ds(o, cbk), :]
            send_row[k, 1, pl.ds(f * cbk, cbk), :] = src[pl.ds(o + (rows - 1) * cbk, cbk), :]
            send_col[k, 0, pl.ds(f * rows, rows), :] = src[pl.ds(o, rows, stride=cbk), :]
            send_col[k, 1, pl.ds(f * rows, rows), :] = src[pl.ds(o + cbk - 1, rows, stride=cbk), :]

    def layer(k, side, count, rows, send_row, recv_row, send_col, recv_col, ss, rs, device):
        back = side ^ 1
        if side < 2:
            m = count * cbk
            return remote(send_row.at[k, back, pl.ds(0, m)], recv_row.at[k, side, pl.ds(0, m)],
                          ss.at[k, back], rs.at[k, side], device)
        m = count * rows
        return remote(send_col.at[k, back - 2, pl.ds(0, m)], recv_col.at[k, side - 2, pl.ds(0, m)],
                      ss.at[k, back], rs.at[k, side], device)

    def start(k, count, rows, *bufs):
        for to in range(4):
            @pl.when(has[to])
            def _():
                layer(k, to ^ 1, count, rows, *bufs, dev[to]).start()

    def arrive(k, count, rows, *bufs):
        for side in range(4):
            @pl.when(has[side])
            def _():
                layer(k, side, count, rows, *bufs, dev[side]).wait_recv()

    def finish(k, count, rows, *bufs):
        for to in range(4):
            @pl.when(has[to])
            def _():
                layer(k, to ^ 1, count, rows, *bufs, dev[to]).wait_send()

    fine = (srow, rrow, scol, rcol, ssem, rsem)
    cvis = (vbox, vbsend, vbrecv)
    coarse = (rbox, rbsend, rbrecv)

    pack(0, vel, 0, 3, rb, srow, scol)
    pack(0, visc, 3, 1, rb, srow, scol)
    for c in range(3):
        sdiag[pl.ds(c * cbk, cbk), :] = vel[pl.ds(c * rb * cbk, cbk), :]

    def pair_lane(x):
        return x + jnp.where(lane % 2 == 0, pltpu.roll(x, lev - 1, 2), pltpu.roll(x, 1, 2))

    def pair_sub(x):
        return x + jnp.where(sub % 2 == 0, pltpu.roll(x, cbk - 1, 1), pltpu.roll(x, 1, 1))

    vis = block(visc, 0, rb)
    vis_rows = vis.reshape(hr, 2, cbk, lev)
    vis_rows = vis_rows[:, 0] + vis_rows[:, 1]
    vis_rc = pair_sub(vis_rows)
    vis_rl = pair_lane(vis_rows)
    cvisc = 0.125 * pair_lane(vis_rc)
    ends = 0.25 * vis_rc
    marked = jnp.where(lane == 1, pltpu.roll(ends, 1, 2),
                       jnp.where(lane == lev - 2, pltpu.roll(ends, lev - 1, 2), cvisc))
    put(halo_v, 0, hr, marked)
    put(chalo_v, 0, hr, 0.25 * vis_rl)
    for j in range(cw):
        vbox[home, pl.ds(j * hr, hr), :] = halo_v[pl.ds(2 * j, hr, stride=cbk), :]
    vbox[home, pl.ds((cw + 1) * hr, hr), :] = cond(
        has[2], chalo_v[pl.ds(cbk - 1, hr, stride=cbk), :], chalo_v[pl.ds(0, hr, stride=cbk), :])
    edge = cond(has[0], 0.25 * pair_lane(pair_sub(vis[rb - 1:]))[0], 0.25 * pair_lane(pair_sub(vis[:1]))[0])
    vbox[home, pl.ds(cw * hr, cbk), :] = edge
    cvreg[...] = jnp.ones(cvreg.shape, jnp.float32)
    for (dl, dc), there in zip(offsets, around):
        @pl.when(jnp.logical_not(there))
        def _():
            rbox[box_index(dl, dc)] = jnp.zeros(rbox.shape[1:], jnp.float32)

    signals = sum(there.astype(jnp.int32) for there in around) + n
    pl.semaphore_wait(barrier, signals)

    start(0, 4, rb, *fine)

    def diagonal_copy(device):
        return remote(sdiag, rdiag, dsem.at[0], dsem.at[1], device)

    @pl.when(has_ul)
    def _():
        diagonal_copy(dev_ul).start()


    vr, vc = rb + 1, 2 * cbk
    for c in range(3):
        for r in range(rb):
            view[pl.ds((c * vr + r) * vc, cbk), :] = vel[pl.ds((c * rb + r) * cbk, cbk), :]

    arrive(0, 4, rb, *fine)

    @pl.when(has_dr)
    def _():
        diagonal_copy(dev_dr).wait_recv()

    zero_row = jnp.zeros((cbk, lev), jnp.float32)
    zero_col = jnp.zeros((rb, lev), jnp.float32)
    for c in range(3):
        view[pl.ds((c * vr + rb) * vc, cbk), :] = cond(
            has[1], rrow[0, 1, pl.ds(c * cbk, cbk), :], zero_row)
        view[pl.ds((c * vr + rb) * vc + cbk, cbk), :] = cond(
            has_dr, rdiag[pl.ds(c * cbk, cbk), :], zero_row)
        view[pl.ds(c * vr * vc + cbk, rb, stride=vc), :] = cond(
            has[3], rcol[0, 1, pl.ds(c * rb, rb), :], zero_col)

    for s in range(q):
        base = rows_in[s] * vc + cols_in[s]
        w = [weights[k, s] for k in range(4)]
        for c in range(3):
            o = base + c * vr * vc
            mixed[pl.ds(s * 3 + c, 1), :] = (
                w[0] * view[pl.ds(o, 1), :] + w[1] * view[pl.ds(o + vc, 1), :]
                + w[2] * view[pl.ds(o + 1, 1), :] + w[3] * view[pl.ds(o + vc + 1, 1), :])
    mixed[pl.ds(q * 3, qrows - q * 3), :] = jnp.zeros((qrows - q * 3, lev), jnp.float32)

    def slot_copy(t, source):
        return remote(mixed, gathered.at[pl.ds(pl.multiple_of(source * qrows, 8), qrows)],
                      gsend.at[t], grecv.at[source],
                      {"patch": other, "lat": t // nlon, "lon": lax.rem(t, nlon)})

    def send_slots(k, _):
        slot_copy(lax.rem(me + k, n), me).start()
        return 0

    lax.fori_loop(0, n, send_slots, 0)

    v_up = cond(has[0], rrow[0, 0, pl.ds(3 * cbk, cbk), :], visc[pl.ds(0, cbk), :])
    v_dn = cond(has[1], rrow[0, 1, pl.ds(3 * cbk, cbk), :], visc[pl.ds((rb - 1) * cbk, cbk), :])
    halo[pl.ds(0, rb, stride=cbk), :] = cond(
        has[2], rcol[0, 0, pl.ds(3 * rb, rb), :], scol[0, 0, pl.ds(3 * rb, rb), :])
    halo[pl.ds(cbk - 1, rb, stride=cbk), :] = cond(
        has[3], rcol[0, 1, pl.ds(3 * rb, rb), :], scol[0, 1, pl.ds(3 * rb, rb), :])

    def stack(x, above, below):
        return (jnp.concatenate([above[None], x[:-1]], axis=0),
                jnp.concatenate([x[1:], below[None]], axis=0))

    def beside(x, h):
        return (jnp.where(sub == 0, h, pltpu.roll(x, 1, 1)),
                jnp.where(sub == cbk - 1, h, pltpu.roll(x, cbk - 1, 1)))

    up, dn = stack(vis, v_up, v_dn)
    lf, rt = beside(vis, block(halo, 0, rb))
    bot = jnp.where(lane == 0, vis, pltpu.roll(vis, 1, 2))
    top = jnp.where(lane == lev - 1, vis, pltpu.roll(vis, lev - 1, 2))
    six = [0.5 * (vis + x) for x in (up, dn, lf, rt, bot, top)]
    diag = six[0] + six[1] + six[2] + six[3] + six[4] + six[5]
    inv = 1.0 / diag
    six[4] = jnp.where(lane == 0, 0.0, six[4])
    six[5] = jnp.where(lane == lev - 1, 0.0, six[5])
    for k in range(6):
        put(cf, k, rb, six[k] * inv)
    put(cf, 6, rb, diag)
    for c in range(3):
        put(ff, c, rb, block(force, c, rb) * inv)
        put(v, c, rb, block(vel, c, rb))

    cols, rows_r = cvreg.shape[0], cvreg.shape[1]
    first_col, first_row = near_lon * cw, near_lat * hr

    def coarse_coefficients():
        box_arrive(*cvis)
        for dl, dc in offsets + [(0, 0)]:
            @pl.when(exists(dl, dc))
            def _():
                for j in range(cw):
                    cvreg[(dc + near_lon) * cw + j, pl.ds((dl + near_lat) * hr, hr), :] = (
                        vbox[box_index(dl, dc), pl.ds(j * hr, hr), :])
        for dc in range(-near_lon, near_lon + 1):
            for at_edge, row in ((lat == 0, first_row - 1), (lat == nlat - 1, first_row + hr)):
                @pl.when(at_edge & exists(0, dc))
                def _():
                    for j in range(cw):
                        cvreg[(dc + near_lon) * cw + j, pl.ds(row, 1), :] = (
                            vbox[box_index(0, dc), pl.ds(cw * hr + 2 * j, 1), :])
        for dc in range(-near_lon, near_lon + 1):
            for at_edge, col in ((lon + dc == 0, (dc + near_lon) * cw - 1),
                                 (lon + dc == nlon - 1, (dc + near_lon + 1) * cw)):
                if 0 <= col < cols:
                    for dl in range(-near_lat, near_lat + 1):
                        @pl.when(at_edge & exists(dl, dc))
                        def _():
                            cvreg[col, pl.ds((dl + near_lat) * hr, hr), :] = (
                                vbox[box_index(dl, dc), pl.ds((cw + 1) * hr, hr), :])
        lane_r = lax.broadcasted_iota(jnp.int32, (1, rows_r, lev), 2)
        row_r = lat * hr - first_row + lax.broadcasted_iota(jnp.int32, (1, rows_r, lev), 1)
        rows_ok = (row_r >= 0) & (row_r < nlat * hr)

        def whole(x):
            return jnp.where(lane_r == 1, pltpu.roll(x, 1, 2),
                             jnp.where(lane_r == lev - 2, pltpu.roll(x, lev - 1, 2), x))

        for col in range(1, cols - 1):
            m = cvreg[pl.ds(col, 1)]
            mid = whole(m)
            cbot = jnp.where(lane_r == 0, pltpu.roll(m, lev - 1, 2), jnp.where(lane_r == 1, m, pltpu.roll(mid, 2, 2)))
            ctop = jnp.where(lane_r == lev - 1, pltpu.roll(m, 1, 2),
                             jnp.where(lane_r == lev - 2, m, pltpu.roll(mid, lev - 2, 2)))
            csix = [0.125 * (mid + x) for x in (
                pltpu.roll(mid, 1, 1), pltpu.roll(mid, rows_r - 1, 1),
                whole(cvreg[pl.ds(col - 1, 1)]), whole(cvreg[pl.ds(col + 1, 1)]), cbot, ctop)]
            cdiag = csix[0] + csix[1] + csix[2] + csix[3] + csix[4] + csix[5]
            col_g = lon * cw - first_col + col
            inside = ((col_g >= 0) & (col_g < nlon * cw)).astype(jnp.int32)
            keep = rows_ok & (jnp.full(rows_ok.shape, inside) == 1)
            cinv = jnp.where(keep, RELAX / cdiag, 0.0)
            csix[4] = jnp.where(lane_r < 2, 0.0, csix[4])
            csix[5] = jnp.where(lane_r >= lev - 2, 0.0, csix[5])
            for k in range(6):
                cc[k, pl.ds(col, 1)] = csix[k] * cinv
            cc[6, pl.ds(col, 1)] = cinv

    def slots_arrive(k, _):
        slot_copy(k, k).wait_recv()
        return 0

    lax.fori_loop(0, n, slots_arrive, 0)
    lon_cells = nlon * cbk
    lat_cells = nlat * rb

    def fetch(first, count, out, side):
        for j in range(count):
            s = slots[first + j]
            d = s // q
            base = d * qrows + (s - d * q) * 3
            for c in range(3):
                out[side, pl.ds(c * count + j, 1), :] = gathered[pl.ds(base + c, 1), :]

    for side, first, count, out in (
            (0, lon * cbk, cbk, grow), (1, lon_cells + lon * cbk, cbk, grow),
            (2, 2 * lon_cells + lat * rb, rb, gcol), (3, 2 * lon_cells + lat_cells + lat * rb, rb, gcol)):
        @pl.when(jnp.logical_not(has[side]))
        def _():
            fetch(first, count, out, side % 2)

    parity = lax.rem(lat * rb + lon * cbk, 2) + lax.broadcasted_iota(jnp.int32, (rb, cbk, lev), 0) + sub + lane
    parity = parity % 2

    def halos(k):
        above, below = [], []
        for c in range(3):
            r = pl.ds(c * cbk, cbk)
            above.append(cond(has[0], rrow[k, 0, r, :], grow[0, r, :]))
            below.append(cond(has[1], rrow[k, 1, r, :], grow[1, r, :]))
            m = pl.ds(c * rb, rb)
            o = c * rb * cbk
            halo[pl.ds(o, rb, stride=cbk), :] = cond(has[2], rcol[k, 0, m, :], gcol[0, m, :])
            halo[pl.ds(o + cbk - 1, rb, stride=cbk), :] = cond(has[3], rcol[k, 1, m, :], gcol[1, m, :])
        return above, below

    def jacobi(x, c, above, below, h, coefs, rows, near, step):
        up, dn = stack(x, above, below)
        lf, rt = near(x, h)
        total = block(coefs, 0, rows) * up + block(coefs, 1, rows) * dn
        total = total + block(coefs, 2, rows) * lf + block(coefs, 3, rows) * rt
        total = total + block(coefs, 4, rows) * pltpu.roll(x, step, 2)
        return total + block(coefs, 5, rows) * pltpu.roll(x, lev - step, 2)

    rounds = 2 * SWEEPS
    for k in range(rounds):
        if k > 0:
            arrive(k, 3, rb, *fine)
        above, below = halos(k)
        for c in range(3):
            x = block(v, c, rb)
            relaxed = block(ff, c, rb) + jacobi(x, c, above[c], below[c], block(halo, c, rb), cf, rb, beside, 1)
            put(v, c, rb, jnp.where(parity == k % 2, relaxed, x))
        pack(k + 1, v, 0, 3, rb, srow, scol)
        start(k + 1, 3, rb, *fine)
        if k == 0:
            box_start(*cvis)
        if k == 2 * SWEEPS - 2:
            coarse_coefficients()
    arrive(rounds, 3, rb, *fine)
    above, below = halos(rounds)
    for c in range(3):
        x = block(v, c, rb)
        relaxed = block(ff, c, rb) + jacobi(x, c, above[c], below[c], block(halo, c, rb), cf, rb, beside, 1)
        residual = block(cf, 6, rb) * (relaxed - x)
        put(res_out, c, rb, residual)
        pairs = residual.reshape(hr, 2, cbk, lev)
        rhs = 0.125 * pair_lane(pair_sub(pairs[:, 0] + pairs[:, 1]))
        put(ce, c, hr, rhs)
        for j in range(cw // 2):
            first = ce[pl.ds(c * hr * cbk + 2 * j, hr, stride=cbk), :]
            second = ce[pl.ds(c * hr * cbk + 2 * (j + cw // 2), hr, stride=cbk), :]
            rbox[home, pl.ds((c * (cw // 2) + j) * hr, hr), :] = jnp.where(lane[0] % 2 == 0, first, second)
    box_start(*coarse)
    box_arrive(*coarse)
    for dl in range(-near_lat, near_lat + 1):
        for dc in range(-near_lon, near_lon + 1):
            r = pl.ds((dl + near_lat) * hr, hr)
            for c in range(3):
                for j in range(cw // 2):
                    both = rbox[box_index(dl, dc), pl.ds((c * (cw // 2) + j) * hr, hr), :]
                    col = (dc + near_lon) * cw + j
                    rhs_reg[c, col, r, :] = jnp.where(lane[0] % 2 == 0, both, pltpu.roll(both, 1, 1))
                    rhs_reg[c, col + cw // 2, r, :] = jnp.where(lane[0] % 2 == 0, pltpu.roll(both, lev - 1, 1), both)
    for c in range(3):
        for col in range(1, cols - 1):
            e = rhs_reg[c, col] * cc[6, col]
            rhs_reg[c, col] = e
            err_reg[c, col] = e
    for k in range(COARSE - 1):
        depth = COARSE - 2 - k
        lo, hi = first_col - depth, first_col + cw + depth
        for c in range(3):
            x = err_reg[c, pl.ds(lo - 1, hi - lo + 2)]
            mid = x[1:-1]
            w = pl.ds(lo, hi - lo)
            total = rhs_reg[c, w] + (1.0 - RELAX) * mid
            total = total + cc[0, w] * pltpu.roll(mid, 1, 1) + cc[1, w] * pltpu.roll(mid, rows_r - 1, 1)
            total = total + cc[2, w] * x[:-2] + cc[3, w] * x[2:]
            total = total + cc[4, w] * pltpu.roll(mid, 2, 2) + cc[5, w] * pltpu.roll(mid, lev - 2, 2)
            err_reg[c, w] = total
    for c in range(3):
        for j in range(cw):
            tile = err_reg[c, first_col + j, pl.ds(first_row, hr), :]
            for twin in range(2):
                ce[pl.ds(c * hr * cbk + 2 * j + twin, hr, stride=cbk), :] = tile

    for c in range(3):
        e = block(ce, c, hr)
        e = jnp.broadcast_to(e[:, None], (hr, 2, cbk, lev)).reshape(rb, cbk, lev)
        put(new_out, c, rb, block(v, c, rb) + e)

    finish(0, 4, rb, *fine)
    for k in range(rounds):
        finish(k + 1, 3, rb, *fine)
    box_finish(*cvis)
    box_finish(*coarse)

    @pl.when(has_ul)
    def _():
        diagonal_copy(dev_ul).wait_send()

    def slots_sent(k, _):
        slot_copy(k, me).wait_send()
        return 0

    lax.fori_loop(0, n, slots_sent, 0)


def per_device(velocity, forcing, viscosity, ghost_slots, corner_rows, corner_cols, corner_weights):
    _, _, rb, cbk, lev = velocity.shape
    nlat, nlon = lax.axis_size("lat"), lax.axis_size("lon")
    n = nlat * nlon
    q = corner_rows.shape[-1]
    qrows = -(-3 * q // 8) * 8 + (8 if (3 * q) % 8 == 0 else 0)
    hr = rb // 2
    flat = rb * cbk
    rounds = 2 * SWEEPS + 1
    f32 = jnp.float32
    vm = lambda *shape: pltpu.VMEM(shape, f32)
    dma = lambda *shape: pltpu.SemaphoreType.DMA(shape)
    vspec = pl.BlockSpec(memory_space=pltpu.VMEM)
    sspec = pl.BlockSpec(memory_space=pltpu.SMEM)
    cw = cbk // 2
    near_lat, near_lon = box_reach(hr, cw)
    nbox = (2 * near_lat + 1) * (2 * near_lon + 1)
    cols, rows_r = (2 * near_lon + 1) * cw, (2 * near_lat + 1) * hr
    new, res = pl.pallas_call(
        functools.partial(kernel, (rb, cbk, lev, nlat, nlon, q, qrows)),
        out_shape=[jax.ShapeDtypeStruct((3 * flat, lev), f32)] * 2,
        in_specs=[vspec] * 3 + [sspec] * 4,
        out_specs=[vspec] * 2,
        scratch_shapes=[
            vm(3 * flat, lev), vm(3 * flat, lev), vm(7 * flat, lev), vm(3 * flat, lev), vm(flat, lev),
            vm(rounds, 2, 4 * cbk, lev), vm(rounds, 2, 4 * cbk, lev),
            vm(rounds, 2, 4 * rb, lev), vm(rounds, 2, 4 * rb, lev),
            dma(rounds, 4), dma(rounds, 4),
            vm(3 * cbk, lev), vm(3 * cbk, lev), dma(2),
            vm(3 * (rb + 1) * 2 * cbk, lev), vm(qrows, lev), vm(n * qrows, lev), dma(n), dma(n),
            vm(2, 3 * cbk, lev), vm(2, 3 * rb, lev),
            vm(nbox, (cw + 2) * hr, lev), dma(nbox), dma(nbox), vm(nbox, 3 * cw // 2 * hr, lev), dma(nbox), dma(nbox),
            vm(3 * hr * cbk, lev), vm(hr * cbk, lev), vm(cols, rows_r, lev), vm(7, cols, rows_r, lev),
            vm(3, cols, rows_r, lev), vm(3, cols, rows_r, lev),
        ],
        compiler_params=pltpu.CompilerParams(
            collective_id=0, has_side_effects=True, vmem_limit_bytes=32 * 2**20),
    )(velocity.reshape(3 * flat, lev), forcing.reshape(3 * flat, lev), viscosity.reshape(flat, lev),
      ghost_slots[0], corner_rows.reshape(q), corner_cols.reshape(q), corner_weights.reshape(4, q))
    return new.reshape(velocity.shape), res.reshape(velocity.shape)


def solution(mesh):
    placed = (
        P("patch", None, "lat", "lon", None),
        P("patch", None, "lat", "lon", None),
        P("patch", "lat", "lon", None),
        P("patch", None),
        P("patch", "lat", "lon"),
        P("patch", "lat", "lon"),
        P("patch", "lat", None, "lon"),
    )
    return jax.shard_map(
        per_device,
        mesh=mesh,
        in_specs=placed,
        out_specs=(P("patch", None, "lat", "lon", None), P("patch", None, "lat", "lon", None)),
        check_vma=False,
    )
```
